32 devices in a mesh: users: 8 (over z, x), panel: 4 (over y, core).
Axes of the slice: x: 2, y: 2, z: 4, core: 2. Of those that a mesh axis runs over, the one named last changes fastest.
Arguments:
- user_emb0: float32 [8192, 128], P('users'), may hold values from -6 to 6
- item_base: float32 [4, 1024, 128], P('panel'), may hold values from -6 to 6
- weight_tiles: bfloat16 [64, 128, 128], replicated, may hold values from -0.02734375 to 0.02734375
- blk_user: int32 [8, 4, 384], P('users', 'panel'), may hold values from 0 to 7
- blk_item: int32 [8, 4, 384], P('users', 'panel'), may hold values from 0 to 7
- blk_weight: int32 [8, 4, 384], P('users', 'panel'), may hold values from 0 to 63
Outputs:
- user_out: float32 [8192, 128], P('users')
- item_emb: float32 [4, 1024, 128], P('panel', 'users')
The draws below stay inside these ranges and needn't reach their ends.
All inputs are finite; a program needn't handle non-finite values.
Results may differ from the reference program's by a relative error of at most 0.0036.
Values may be sent and summed in bfloat16 or wider, within the bound.
A program may use at most 128 MiB of HBM per device.

```python
import math
import jax
import jax.numpy as jnp
import numpy as np
from jax import lax

E = 128
TILE = 128
UT_DEV = 8
BLK_DEV = 384
NWT = 64
USERS = 8192
ITEMS_PANEL = 1024
N_USERS = 8
N_PANEL = 4


def plant(array, own_key, smallest, top_value):
    longest = array.shape.index(max(array.shape))
    spots = []
    for shift in (0, 1):
        where = [jax.random.randint(jax.random.fold_in(own_key, axis), (), 0, length) for axis, length in enumerate(array.shape)]
        where[longest] = (where[longest] + shift) % array.shape[longest]
        spots.append(tuple(where))
    return array.at[spots[0]].set(smallest).at[spots[1]].set(top_value)


def shard_levels(rng, shape, cuts, low, top_value):
    def one(dim, shards_of):
        draws = jax.random.uniform(jax.random.fold_in(jax.random.fold_in(rng, 6), dim), (shards_of,), jnp.float32, low / len(cuts), top_value / len(cuts))
        return jnp.repeat(jnp.exp(draws), shape[dim] // shards_of).reshape((-1,) + (1,) * (len(shape) - dim - 1))

    level = one(*cuts[0])
    for cut in cuts[1:]:
        level = level * one(*cut)
    return level


def rank_bounds(amount, lean):
    loads = [(1 << 20) // math.isqrt(rank ** lean) + 1 for rank in range(1, amount + 1)]
    spread = 1 + sum(loads) // (1 << 30)
    return np.cumsum(np.array([max(1, weight // spread) for weight in loads]))


def ranked_ids(own_key, extent, amount, slope):
    listing = rank_bounds(amount, slope)
    ticket = jax.random.randint(jax.random.fold_in(own_key, 1), extent, 0, int(listing[amount - 1]))
    rank = jnp.searchsorted(jnp.asarray(listing, jnp.int32), ticket, side="right")
    return jax.random.permutation(jax.random.fold_in(own_key, 2), amount)[rank].astype(jnp.int32)


def noise(stream_key, dims, width, reach, split=(), held_as=jnp.bfloat16):
    entries = jax.random.normal(stream_key, dims, jnp.float32) * width
    if len(split) > 0:
        entries = shard_levels(stream_key, dims, split, -0.22, 0.18) * entries
    return jnp.clip(entries, min=-reach, max=reach).astype(held_as)


def setup_inputs(seed: int = 0) -> dict:
    splits = jax.random.split(jax.random.key(seed), 7)
    return {
        "user_emb0": noise(splits[0], (USERS, E), 1.0, 6.0, ((0, 8),), jnp.float32),
        "item_base": noise(splits[1], (N_PANEL, ITEMS_PANEL, E), 1.0, 6.0, ((0, 4),), jnp.float32),
        "weight_tiles": noise(splits[2], (NWT, TILE, TILE), (TILE * BLK_DEV) ** -0.5, 0.02734375),
        "blk_user": plant(jax.random.randint(splits[3], (N_USERS, N_PANEL, BLK_DEV), 0, UT_DEV), jax.random.fold_in(splits[3], 1), 0, UT_DEV - 1).astype(jnp.int32),
        "blk_item": plant(ranked_ids(splits[4], (N_USERS, N_PANEL, BLK_DEV), N_USERS, 2), jax.random.fold_in(splits[4], 3), 0, N_USERS - 1).astype(jnp.int32),
        "blk_weight": plant(jax.random.randint(splits[5], (N_USERS, N_PANEL, BLK_DEV), 0, NWT), jax.random.fold_in(splits[5], 1), 0, NWT - 1).astype(jnp.int32),
    }


teleport = 0.2


def item_terms(user_tiles, users, items, weights, weight_tiles, n_items):
    group_size = min(users.shape[0], 128)
    pieces = (users.reshape(-1, group_size), items.reshape(-1, group_size), weights.reshape(-1, group_size))

    def add_group(totals, lists):
        tiles = weight_tiles[lists[2]].astype(jnp.float32)
        rows = user_tiles[lists[0]].astype(jnp.float32)
        products = jnp.einsum("gab,gae->gbe", tiles, rows)
        return totals + jax.ops.segment_sum(products, lists[1], num_segments=n_items), None

    start = jnp.zeros((n_items, user_tiles.shape[1], user_tiles.shape[2]), jnp.float32)
    totals, unused = lax.scan(add_group, start, pieces)
    return totals


def user_terms(item_tiles, users, items, weights, weight_tiles, n_tiles):
    group_size = min(users.shape[0], 128)
    pieces = (users.reshape(-1, group_size), items.reshape(-1, group_size), weights.reshape(-1, group_size))

    def add_group(totals, lists):
        tiles = weight_tiles[lists[2]].astype(jnp.float32)
        rows = item_tiles[lists[1]].astype(jnp.float32)
        products = jnp.einsum("gab,gbe->gae", tiles, rows)
        return totals + jax.ops.segment_sum(products, lists[0], num_segments=n_tiles), None

    start = jnp.zeros((n_tiles, item_tiles.shape[1], item_tiles.shape[2]), jnp.float32)
    totals, unused = lax.scan(add_group, start, pieces)
    return totals


def reference(user_emb0, item_base, weight_tiles, blk_user, blk_item, blk_weight):
    user_bf = user_emb0.astype(jnp.bfloat16).reshape(N_USERS, UT_DEV, TILE, E)

    def item_device(totals, device):
        user_local = device[0]

        def one_panel(lists):
            return item_terms(user_local, lists[0], lists[1], lists[2], weight_tiles, N_USERS)

        terms = lax.map(one_panel, (device[1], device[2], device[3]))
        return totals + terms, None

    start = jnp.zeros((N_PANEL, N_USERS, TILE, E), jnp.float32)
    item_sum, unused = lax.scan(item_device, start, (user_bf, blk_user, blk_item, blk_weight))
    item_emb = (1.0 - teleport) * item_sum.reshape(N_PANEL, N_USERS * TILE, E) + teleport * item_base
    item_bf = item_emb.astype(jnp.bfloat16).reshape(N_PANEL, N_USERS, TILE, E)

    def user_device(device):
        def one_panel(lists):
            return user_terms(lists[0], lists[1], lists[2], lists[3], weight_tiles, UT_DEV)

        terms = lax.map(one_panel, (item_bf, device[0], device[1], device[2]))
        return jnp.sum(terms, axis=0)

    user_sum = lax.map(user_device, (blk_user, blk_item, blk_weight))
    user_out = (1.0 - teleport) * user_sum.reshape(USERS, E) + teleport * user_emb0
    return user_out, item_emb
```

```python
import functools

import jax
import jax.numpy as jnp
from jax import lax
from jax.experimental import pallas as pl
from jax.experimental.pallas import tpu as pltpu
from jax.sharding import PartitionSpec as P

teleport = 0.2
ITEM_GROUP = 8
MESH = pl.DeviceIdType.MESH


def sum_weights(n_blocks, n_items, group, tile, users, items, weights, tiles, out, acc):
    n_user_tiles = out.shape[1] // tile
    first = pl.program_id(0) * group
    acc[...] = jnp.zeros_like(acc)

    def add(k, carry):
        i = items[k] - first

        def go():
            slot = i * n_user_tiles + users[k]
            acc[slot] += tiles[weights[k]].astype(jnp.float32)

        if group == n_items:
            go()
        else:
            pl.when((i >= 0) & (i < group))(go)
        return carry

    lax.fori_loop(0, n_blocks, add, 0, unroll=8)
    for i in range(group):
        for u in range(n_user_tiles):
            out[i, u * tile : (u + 1) * tile, :] = acc[i * n_user_tiles + u].astype(out.dtype)


def run(lo, hi, body):
    if hi - lo <= 8:
        for s in range(lo, hi):
            body(s)
    else:
        lax.fori_loop(lo, hi, lambda s, c: (body(s), c)[1], 0)


def exchange(
    n, tile, user, base, a, user_out, item_out,
    ut, total, sends, recvs, embs, part, core_send, core_recv, y_send, y_recv,
    s1, r1, s2, r2, s3, r3, s4, r4, s5, r5,
):
    me = lax.axis_index("users")
    panel = lax.axis_index("panel")
    core = lax.rem(panel, 2)
    other = panel + 1 - 2 * core
    across = lax.rem(panel + 2, 4)
    rows = user.shape[0]
    half = rows // 2
    chunks = half // tile

    barrier = pltpu.get_barrier_semaphore()

    def greet(s):
        pl.semaphore_signal(
            barrier, inc=1, device_id={"users": lax.rem(me + s, n), "panel": panel}, device_id_type=MESH
        )

    run(1, n, greet)
    for p in (other, across):
        pl.semaphore_signal(barrier, inc=1, device_id={"users": me, "panel": p}, device_id_type=MESH)

    ut[...] = jnp.transpose(user[...]).astype(ut.dtype)

    def term(t):
        return jnp.dot(ut[...], a[t], preferred_element_type=jnp.float32)

    total[...] = term(me)
    pl.semaphore_wait(barrier, n + 1)

    def to(s, src, dst, ssem, rsem):
        return pltpu.make_async_remote_copy(
            src_ref=src, dst_ref=dst, send_sem=ssem, recv_sem=rsem,
            device_id={"users": lax.rem(me + s, n), "panel": panel}, device_id_type=MESH,
        )

    def hop(p, src, dst, ssem, rsem):
        return pltpu.make_async_remote_copy(
            src_ref=src, dst_ref=dst, send_sem=ssem, recv_sem=rsem,
            device_id={"users": me, "panel": p}, device_id_type=MESH,
        )

    def partial(s):
        return to(s, sends.at[s], recvs.at[s], s1.at[s], r1.at[s])

    def send_partial(s):
        sends[s] = term(lax.rem(me + s, n)).astype(sends.dtype)
        partial(s).start()

    run(1, n, send_partial)

    def add_partial(s):
        partial(s).wait_recv()
        total[...] += recvs[s].astype(jnp.float32)

    run(1, n, add_partial)
    own = pl.ds(pl.multiple_of(me * tile, tile), tile)
    emb = (1.0 - teleport) * jnp.transpose(total[...]) + teleport * base[own, :]
    item_out[...] = emb
    embs[me] = emb.astype(embs.dtype)

    def spread(s):
        to(s, embs.at[me], embs.at[me], s2.at[s], r2.at[s]).start()

    run(1, n, spread)
    part[...] = jnp.dot(a[me], embs[me], preferred_element_type=jnp.float32)

    def use(s):
        j = lax.rem(me - s + n, n)
        to(s, embs.at[j], embs.at[j], s2.at[s], r2.at[s]).wait_recv()
        part[...] += jnp.dot(a[j], embs[j], preferred_element_type=jnp.float32)

    run(1, n, use)

    mine = core * half
    theirs = half - mine

    def to_core(k):
        return hop(other, core_send.at[k], core_recv.at[k], s3.at[k], r3.at[k])

    def to_y(k):
        return hop(across, y_send.at[k], y_recv.at[k], s4.at[k], r4.at[k])

    def back(k):
        where = pl.ds(pl.multiple_of(mine + k * tile, tile), tile)
        return hop(other, user_out.at[where, :], user_out.at[where, :], s5.at[k], r5.at[k])

    def back_recv(k):
        where = pl.ds(pl.multiple_of(theirs + k * tile, tile), tile)
        return hop(other, user_out.at[where, :], user_out.at[where, :], s5.at[k], r5.at[k])

    for k in range(chunks):
        core_send[k] = part[pl.ds(pl.multiple_of(theirs + k * tile, tile), tile), :].astype(core_send.dtype)
        to_core(k).start()
    for k in range(chunks):
        to_core(k).wait_recv()
        where = pl.ds(pl.multiple_of(mine + k * tile, tile), tile)
        y_send[k] = (part[where, :] + core_recv[k].astype(jnp.float32)).astype(y_send.dtype)
        to_y(k).start()
    for k in range(chunks):
        to_y(k).wait_recv()
        where = pl.ds(pl.multiple_of(mine + k * tile, tile), tile)
        both = y_send[k].astype(jnp.float32) + y_recv[k].astype(jnp.float32)
        user_out[where, :] = (1.0 - teleport) * both + teleport * user[where, :]
        back(k).start()

    def drain(s):
        partial(s).wait_send()
        to(s, embs.at[me], embs.at[me], s2.at[s], r2.at[s]).wait_send()

    run(1, n, drain)
    for k in range(chunks):
        to_core(k).wait_send()
        to_y(k).wait_send()
        back(k).wait_send()
        back_recv(k).wait_recv()


def per_device(user_emb0, item_base, weight_tiles, blk_user, blk_item, blk_weight):
    n = lax.axis_size("users")
    n_weights, tile, width = weight_tiles.shape[0], weight_tiles.shape[1], user_emb0.shape[1]
    rows = user_emb0.shape[0]
    n_user_tiles = rows // tile
    n_items = item_base.shape[1] // tile
    n_blocks = blk_user.shape[-1]
    group = min(n_items, ITEM_GROUP)
    smem = pl.BlockSpec(memory_space=pltpu.SMEM)
    vmem = pl.BlockSpec(memory_space=pltpu.VMEM)
    bf, f32 = jnp.bfloat16, jnp.float32
    dma = pltpu.SemaphoreType.DMA

    a = pl.pallas_call(
        functools.partial(sum_weights, n_blocks, n_items, group, tile),
        grid=(n_items // group,),
        out_shape=jax.ShapeDtypeStruct((n_items, rows, tile), bf),
        in_specs=[smem, smem, smem, vmem],
        out_specs=pl.BlockSpec((group, rows, tile), lambda g: (g, 0, 0)),
        scratch_shapes=[pltpu.VMEM((group * n_user_tiles, tile, tile), f32)],
        compiler_params=pltpu.CompilerParams(vmem_limit_bytes=24 << 20),
    )(blk_user.reshape(-1), blk_item.reshape(-1), blk_weight.reshape(-1), weight_tiles)

    chunks = rows // 2 // tile
    user_out, own = pl.pallas_call(
        functools.partial(exchange, n, tile),
        out_shape=(
            jax.ShapeDtypeStruct((rows, width), f32),
            jax.ShapeDtypeStruct((tile, width), f32),
        ),
        in_specs=[vmem] * 3,
        out_specs=(vmem, vmem),
        scratch_shapes=[
            pltpu.VMEM((width, rows), bf),
            pltpu.VMEM((width, tile), f32),
            pltpu.VMEM((n, width, tile), bf),
            pltpu.VMEM((n, width, tile), bf),
            pltpu.VMEM((n, tile, width), bf),
            pltpu.VMEM((rows, width), f32),
            pltpu.VMEM((chunks, tile, width), bf),
            pltpu.VMEM((chunks, tile, width), bf),
            pltpu.VMEM((chunks, tile, width), bf),
            pltpu.VMEM((chunks, tile, width), bf),
        ]
        + [dma((n,))] * 4
        + [dma((chunks,))] * 6,
        compiler_params=pltpu.CompilerParams(
            collective_id=0, has_side_effects=True, vmem_limit_bytes=48 << 20
        ),
    )(user_emb0, item_base[0], a)
    return user_out, own[None]


def solution(mesh):
    placed = (
        P("users", None),
        P("panel", None, None),
        P(),
        P("users", "panel", None),
        P("users", "panel", None),
        P("users", "panel", None),
    )
    return jax.shard_map(
        per_device,
        mesh=mesh,
        in_specs=placed,
        out_specs=(P("users", None), P("panel", "users", None)),
        check_vma=False,
    )
```

```python
import functools

import jax
import jax.numpy as jnp
from jax import lax
from jax.experimental import pallas as pl
from jax.experimental.pallas import tpu as pltpu
from jax.sharding import PartitionSpec as P

teleport = 0.2
ITEM_GROUP = 8
HALVES = 1
CUTS = 2
MESH = pl.DeviceIdType.MESH


def sum_weights(n_blocks, n_items, group, tile, listed, tiles, out, acc):
    n_user_tiles = out.shape[1] // tile
    first = pl.program_id(0) * group
    acc[...] = jnp.zeros_like(acc)

    def add(k, carry):
        pair = lax.div(listed[k], tiles.shape[0])
        slot = pair - first * n_user_tiles
        w = listed[k] - pair * tiles.shape[0]

        def go():
            acc[slot] += tiles[w].astype(jnp.float32)

        if group == n_items:
            go()
        else:
            pl.when((slot >= 0) & (slot < group * n_user_tiles))(go)
        return carry

    lax.fori_loop(0, n_blocks, add, 0, unroll=8)
    for i in range(group):
        for u in range(n_user_tiles):
            out[i, u * tile : (u + 1) * tile, :] = acc[i * n_user_tiles + u].astype(out.dtype)


def run(lo, hi, body):
    if hi - lo <= 8:
        for s in range(lo, hi):
            body(s)
    else:
        lax.fori_loop(lo, hi, lambda s, c: (body(s), c)[1], 0)


def exchange(
    n, tile, user, base, a, user_out, item_out,
    ut, base_t, total, emb_t, sends, recvs, embs, part, core_send, core_recv, y_send, y_recv, done,
    s1, r1, s2, r2, s3, r3, s4, r4, s5, r5,
):
    me = lax.axis_index("users")
    panel = lax.axis_index("panel")
    core = lax.rem(panel, 2)
    other = panel + 1 - 2 * core
    across = lax.rem(panel + 2, 4)
    cuts, cols = part.shape[1], part.shape[3]
    half = cuts * cols
    depth = total.shape[0] // HALVES

    def peer(s):
        return {"users": lax.rem(me + s, n), "panel": panel}

    def hop(where, src, dst, ssem, rsem):
        return pltpu.make_async_remote_copy(
            src_ref=src, dst_ref=dst, send_sem=ssem, recv_sem=rsem, device_id=where, device_id_type=MESH
        )

    barrier = pltpu.get_barrier_semaphore()

    def greet(where):
        pl.semaphore_signal(barrier, inc=1, device_id=where, device_id_type=MESH)

    run(1, n, lambda s: greet(peer(s)))
    greet({"users": me, "panel": other})
    greet({"users": me, "panel": across})

    ut[...] = jnp.transpose(user[...]).astype(ut.dtype)
    own = pl.ds(pl.multiple_of(me * tile, tile), tile)
    base_t[...] = teleport * jnp.transpose(base[own, :])

    def term(t):
        return jnp.dot(ut[...], a[t], preferred_element_type=jnp.float32)

    total[...] = term(me)
    pl.semaphore_wait(barrier, n + 1)

    def deep(h):
        return pl.ds(h * depth, depth)

    def partial(h, s):
        return hop(peer(s), sends.at[s, deep(h)], recvs.at[s, deep(h)], s1.at[h, s], r1.at[h, s])

    def spread(h, s, j):
        return hop(peer(s), embs.at[j, deep(h)], embs.at[j, deep(h)], s2.at[h, s], r2.at[h, s])

    def send_partial(s):
        sends[s] = term(lax.rem(me + s, n)).astype(sends.dtype)
        partial(0, s).start()

    run(1, n, send_partial)
    for h in range(1, HALVES):
        run(1, n, lambda s: partial(h, s).start())

    def finish_items(h):
        def add_partial(s):
            partial(h, s).wait_recv()
            total[deep(h), :] += recvs[s, deep(h), :].astype(jnp.float32)

        run(1, n, add_partial)
        emb = (1.0 - teleport) * total[deep(h), :] + base_t[deep(h), :]
        emb_t[deep(h), :] = emb
        embs[me, deep(h), :] = emb.astype(embs.dtype)
        run(1, n, lambda s: spread(h, s, me).start())

    def multiply(h, j, first):
        for c in range(2):
            for k in range(cuts):
                rows = pl.ds(c * half + k * cols, cols)
                value = lax.dot_general(
                    embs[j, deep(h), :], a[j, rows, :], (((1,), (1,)), ((), ())),
                    preferred_element_type=jnp.float32,
                )
                part[c, k, deep(h), :] = value if first else part[c, k, deep(h), :] + value

    def use(h, lo, hi):
        def one(s):
            j = lax.rem(me - s + n, n)
            spread(h, s, j).wait_recv()
            multiply(h, j, False)

        run(lo, hi, one)

    def to_core(h, k):
        return hop({"users": me, "panel": other}, core_send.at[h, k], core_recv.at[h, k], s3.at[h, k], r3.at[h, k])

    def to_y(h, k):
        return hop({"users": me, "panel": across}, y_send.at[h, k], y_recv.at[h, k], s4.at[h, k], r4.at[h, k])

    def back(h, k, c):
        where = done.at[c, k, deep(h)]
        return hop({"users": me, "panel": other}, where, where, s5.at[h, k], r5.at[h, k])

    def give_core(h):
        for k in range(cuts):
            core_send[h, k] = part[1 - core, k, deep(h), :].astype(core_send.dtype)
            to_core(h, k).start()

    def give_y(h):
        for k in range(cuts):
            to_core(h, k).wait_recv()
            both = part[core, k, deep(h), :] + core_recv[h, k].astype(jnp.float32)
            y_send[h, k] = both.astype(y_send.dtype)
            to_y(h, k).start()

    def give_back(h):
        for k in range(cuts):
            to_y(h, k).wait_recv()
            done[core, k, deep(h), :] = y_send[h, k].astype(jnp.float32) + y_recv[h, k].astype(jnp.float32)
            back(h, k, core).start()

    def write(c, k):
        where = pl.ds(pl.multiple_of(c * half + k * cols, cols), cols)
        user_out[where, :] = (1.0 - teleport) * jnp.transpose(done[c, k]) + teleport * user[where, :]

    finish_items(0)
    multiply(0, me, True)
    item_out[...] = jnp.transpose(emb_t[...])
    use(0, 1, n)
    give_core(0)
    give_y(0)
    give_back(0)
    for k in range(cuts):
        write(core, k)

    def drain(s):
        for h in range(HALVES):
            partial(h, s).wait_send()
            spread(h, s, me).wait_send()

    run(1, n, drain)
    for k in range(cuts):
        for h in range(HALVES):
            to_core(h, k).wait_send()
            to_y(h, k).wait_send()
            back(h, k, core).wait_send()
            back(h, k, 1 - core).wait_recv()
        write(1 - core, k)


def per_device(user_emb0, item_base, weight_tiles, blk_user, blk_item, blk_weight):
    n = lax.axis_size("users")
    n_weights, tile, width = weight_tiles.shape[0], weight_tiles.shape[1], user_emb0.shape[1]
    rows = user_emb0.shape[0]
    n_user_tiles = rows // tile
    n_items = item_base.shape[1] // tile
    n_blocks = blk_user.shape[-1]
    group = min(n_items, ITEM_GROUP)
    smem = pl.BlockSpec(memory_space=pltpu.SMEM)
    vmem = pl.BlockSpec(memory_space=pltpu.VMEM)
    bf, f32 = jnp.bfloat16, jnp.float32
    dma = pltpu.SemaphoreType.DMA

    a = pl.pallas_call(
        functools.partial(sum_weights, n_blocks, n_items, group, tile),
        grid=(n_items // group,),
        out_shape=jax.ShapeDtypeStruct((n_items, rows, tile), bf),
        in_specs=[smem, vmem],
        out_specs=pl.BlockSpec((group, rows, tile), lambda g: (g, 0, 0)),
        scratch_shapes=[pltpu.VMEM((group * n_user_tiles, tile, tile), f32)],
        compiler_params=pltpu.CompilerParams(vmem_limit_bytes=24 << 20),
    )(((blk_item * n_user_tiles + blk_user) * n_weights + blk_weight).reshape(-1), weight_tiles)

    cols = rows // 2 // CUTS
    user_out, own = pl.pallas_call(
        functools.partial(exchange, n, tile),
        out_shape=(
            jax.ShapeDtypeStruct((rows, width), f32),
            jax.ShapeDtypeStruct((tile, width), f32),
        ),
        in_specs=[vmem] * 3,
        out_specs=(vmem, vmem),
        scratch_shapes=[
            pltpu.VMEM((width, rows), bf),
            pltpu.VMEM((width, tile), f32),
            pltpu.VMEM((width, tile), f32),
            pltpu.VMEM((width, tile), f32),
            pltpu.VMEM((n, width, tile), bf),
            pltpu.VMEM((n, width, tile), bf),
            pltpu.VMEM((n, width, tile), bf),
            pltpu.VMEM((2, CUTS, width, cols), f32),
        ]
        + [pltpu.VMEM((HALVES, CUTS, width // HALVES, cols), bf)] * 4
        + [pltpu.VMEM((2, CUTS, width, cols), f32)]
        + [dma((HALVES, n))] * 4
        + [dma((HALVES, CUTS))] * 6,
        compiler_params=pltpu.CompilerParams(
            collective_id=0, has_side_effects=True, vmem_limit_bytes=48 << 20
        ),
    )(user_emb0, item_base[0], a)
    return user_out, own[None]


def solution(mesh):
    placed = (
        P("users", None),
        P("panel", None, None),
        P(),
        P("users", "panel", None),
        P("users", "panel", None),
        P("users", "panel", None),
    )
    return jax.shard_map(
        per_device,
        mesh=mesh,
        in_specs=placed,
        out_specs=(P("users", None), P("panel", "users", None)),
        check_vma=False,
    )
```
